32 devices in a mesh: section: 8 (over y, x, core), dp: 4 (over z).
Axes of the slice: x: 2, y: 2, z: 4, core: 2. Of those that a mesh axis runs over, the one named last changes fastest.
Arguments:
- stash_q: bfloat16 [8, 4, 128, 4096], P('section', 'dp'), may hold values from -5.5 to 5.5
- stash_kv: bfloat16 [8, 4, 128, 1024], P('section', 'dp'), may hold values from -5.5 to 5.5
- upstream: bfloat16 [8, 4, 128, 4096], P('section', 'dp'), may hold values from -6 to 6
- lengths: int32 [4], P('dp'), may hold values from 2 to 128, as said below
- domains: int32 [4], P('dp'), may hold values from 0 to 6
- domain_weight: float32 [7], replicated, may hold values from 0.3 to 3
Outputs:
- grad_q: bfloat16 [8, 4, 128, 4096], P('section', 'dp')
- grad_kv: bfloat16 [8, 4, 128, 1024], P('section', 'dp')
The draws below stay inside these ranges and needn't reach their ends.
Inputs may be any that keep to these rules, and one draw needn't show every extreme that they name: `lengths`: some micro-batch has exactly 128 live tokens.
All inputs are finite; a program needn't handle non-finite values.
Results may differ from the reference program's by a relative error of at most 0.006.
Values may be sent and summed in bfloat16 or wider, within the bound.
A program may use at most 64 MiB of HBM per device.

```python
import math
import jax
import jax.numpy as jnp
from jax import lax

QUERY_HEADS = 32
KEY_VALUE_HEADS = 4
HEAD_SIZE = 128
DOMAINS = 7
SEQUENCE_TOKENS = 128
MB = 1
RELAY_SECTIONS = 8
MICRO_BATCHES = 4


def draw_stash_q(key, part):
    baseline_loss = jnp.clip(jax.random.normal(jax.random.fold_in(key, 1), (RELAY_SECTIONS, MICRO_BATCHES, SEQUENCE_TOKENS, QUERY_HEADS * HEAD_SIZE), jnp.float32), -4.0, 4.0)
    return baseline_loss.astype(jnp.bfloat16)


def draw_stash_kv(key, part):
    baseline_loss = jnp.clip(jax.random.normal(jax.random.fold_in(key, 2), (RELAY_SECTIONS, MICRO_BATCHES, SEQUENCE_TOKENS, 2 * KEY_VALUE_HEADS * HEAD_SIZE), jnp.float32), -4.0, 4.0)
    return baseline_loss.astype(jnp.bfloat16)


def draw_lengths(key, part):
    replicas = MICRO_BATCHES // MB
    replica = jnp.arange(MICRO_BATCHES, dtype=jnp.int32) // MB
    lower = 2 + (SEQUENCE_TOKENS * 3 // 4 - 2) * replica // max(replicas - 1, 1)
    upper = lower + SEQUENCE_TOKENS // 4 + 1
    upper = jnp.minimum(upper, SEQUENCE_TOKENS + 1)
    drawn = jax.random.randint(jax.random.fold_in(key, 3), (MICRO_BATCHES,), lower, upper).astype(jnp.int32)
    index = jnp.arange(MICRO_BATCHES, dtype=jnp.int32)
    drawn = jnp.where(index == MICRO_BATCHES - 1, SEQUENCE_TOKENS, drawn)
    drawn = jnp.where(index == 0, 2, drawn)
    return drawn.astype(jnp.int32)


def touch_ends(result, stream_key, smallest, high):
    spot = [jax.random.randint(jax.random.fold_in(stream_key, axis), (), 0, length) for axis, length in enumerate(result.shape)]
    longest = result.shape.index(max(result.shape))
    neighbour = spot[:longest] + [(spot[longest] + 1) % result.shape[longest]] + spot[longest + 1:]
    return result.at[tuple(spot)].set(smallest).at[tuple(neighbour)].set(high)


def level_of(own_key, extent, pieces, least, high):
    factor_of, own = 1.0, jax.random.fold_in(own_key, 6)
    for dim, parts in pieces:
        draws = jnp.exp(jax.random.uniform(jax.random.fold_in(own, dim), (parts,), jnp.float32, least / len(pieces), high / len(pieces)))
        factor_of = factor_of * jnp.repeat(draws, extent[dim] // parts).reshape([-1 if axis == dim else 1 for axis in range(len(extent))])
    return factor_of


def centred(stream_key, extent, width, limit, pieces=(), held_as=jnp.bfloat16):
    values = jax.random.normal(stream_key, extent, jnp.float32) * width
    if len(pieces) > 0:
        values = level_of(stream_key, extent, pieces, -0.22, 0.18) * values
    return jnp.clip(values, min=-limit, max=limit).astype(held_as)


def setup_inputs(seed: int = 0) -> dict:
    seeds = jax.random.split(jax.random.key(seed), 7)
    return {
        "stash_q": draw_stash_q(jax.random.fold_in(seeds[6], 71), 0),
        "stash_kv": draw_stash_kv(jax.random.fold_in(seeds[6], 71), 0),
        "upstream": centred(seeds[2], (RELAY_SECTIONS, MICRO_BATCHES, SEQUENCE_TOKENS, QUERY_HEADS * HEAD_SIZE), 1.0, 6.0, ((0, 8), (1, 4))),
        "lengths": draw_lengths(jax.random.fold_in(seeds[6], 71), 0),
        "domains": touch_ends(jax.random.randint(seeds[4], (MICRO_BATCHES,), 0, DOMAINS), jax.random.fold_in(seeds[4], 1), 0, DOMAINS - 1).astype(jnp.int32),
        "domain_weight": jnp.clip(jnp.exp(jax.random.uniform(seeds[5], (DOMAINS,), jnp.float32, math.log(0.3), math.log(3.0))), 0.3, 3.0),
    }


def backward_block(query_rows, paired_stash, grads, lengths, factor):
    batch_list = query_rows.shape[0]
    group_count = QUERY_HEADS // KEY_VALUE_HEADS
    inv_root = 1.0 / math.sqrt(HEAD_SIZE)
    query_head_rows = query_rows.astype(jnp.float32).reshape(batch_list, SEQUENCE_TOKENS, KEY_VALUE_HEADS, group_count, HEAD_SIZE)
    key_head_rows = paired_stash[..., :KEY_VALUE_HEADS * HEAD_SIZE].astype(jnp.float32).reshape(batch_list, SEQUENCE_TOKENS, KEY_VALUE_HEADS, HEAD_SIZE)
    value_head_rows = paired_stash[..., KEY_VALUE_HEADS * HEAD_SIZE:].astype(jnp.float32).reshape(batch_list, SEQUENCE_TOKENS, KEY_VALUE_HEADS, HEAD_SIZE)
    row_index = jnp.arange(SEQUENCE_TOKENS, dtype=jnp.int32)[:, None]
    col_index = jnp.arange(SEQUENCE_TOKENS, dtype=jnp.int32)[None, :]
    allowed = (col_index <= row_index)[None] & (col_index[None] < lengths[:, None, None])
    live = jnp.arange(SEQUENCE_TOKENS, dtype=jnp.int32)[None, :] < lengths[:, None]
    gradient_heads = jnp.where(live[:, :, None], grads, jnp.zeros((), grads.dtype))
    gradient_heads = gradient_heads.astype(jnp.float32).reshape(batch_list, SEQUENCE_TOKENS, KEY_VALUE_HEADS, group_count, HEAD_SIZE)
    scores = jnp.einsum('bikgd,bjkd->bkgij', query_head_rows, key_head_rows) * inv_root
    scores = jnp.where(allowed[:, None, None], scores, jnp.float32(-1e+30))
    peak = lax.optimization_barrier(jnp.max(scores, axis=-1, keepdims=True))
    expo = jnp.exp(scores - peak)
    probability = expo / lax.optimization_barrier(jnp.sum(expo, axis=-1, keepdims=True))
    prob_half = probability.astype(jnp.bfloat16).astype(jnp.float32)
    value_gradient = jnp.einsum('bkgij,bikgd->bjkd', prob_half, gradient_heads)
    prob_grad = jnp.einsum('bikgd,bjkd->bkgij', gradient_heads, value_head_rows)
    row_total = lax.optimization_barrier(jnp.sum(probability * prob_grad, axis=-1, keepdims=True))
    score_grad = (probability * (prob_grad - row_total) * inv_root).astype(jnp.bfloat16).astype(jnp.float32)
    query_grad = jnp.einsum('bkgij,bjkd->bikgd', score_grad, key_head_rows)
    key_gradient = jnp.einsum('bkgij,bikgd->bjkd', score_grad, query_head_rows)
    row_scales = factor[:, None, None]
    out_q = (query_grad.reshape(batch_list, SEQUENCE_TOKENS, QUERY_HEADS * HEAD_SIZE) * row_scales).astype(jnp.bfloat16)
    output_key = key_gradient.reshape(batch_list, SEQUENCE_TOKENS, KEY_VALUE_HEADS * HEAD_SIZE) * row_scales
    output_value = value_gradient.reshape(batch_list, SEQUENCE_TOKENS, KEY_VALUE_HEADS * HEAD_SIZE) * row_scales
    return (out_q, jnp.concatenate([output_key, output_value], axis=-1).astype(jnp.bfloat16))

def reference(stash_q, stash_kv, upstream, lengths, domains, domain_weight):
    domain_ids = jnp.arange(DOMAINS, dtype=jnp.int32)
    onehot = domains[:, None] == domain_ids[None, :]
    counts = lax.optimization_barrier(jnp.sum(jnp.where(onehot, lengths[:, None], 0), axis=0)).astype(jnp.int32)
    count_float = counts.astype(jnp.float32)
    token_total = jnp.sum(count_float)
    own_count = lax.optimization_barrier(jnp.sum(jnp.where(onehot, count_float[None, :], jnp.float32(0.0)), axis=1))
    weight = lax.optimization_barrier(jnp.sum(jnp.where(onehot, domain_weight[None, :], jnp.float32(0.0)), axis=1))
    factor = weight * token_total / (DOMAINS * own_count)
    partner_q = jnp.roll(stash_q, RELAY_SECTIONS // 2, axis=0)
    partner_kv = jnp.roll(stash_kv, RELAY_SECTIONS // 2, axis=0)
    next_grads = jnp.roll(upstream, -1, axis=0)

    def one_section(items):
        return backward_block(items[0], items[1], items[2], lengths, factor)
    grad_q, grad_kv = lax.map(one_section, (partner_q, partner_kv, next_grads))
    return (grad_q, grad_kv)
```

```python
import functools
import math

import jax
import jax.numpy as jnp
from jax import lax
from jax.experimental import pallas as pl
from jax.experimental.pallas import tpu as pltpu
from jax.sharding import PartitionSpec as P

HEAD_SIZE = 128
DOMAINS = 7
MESH = pl.DeviceIdType.MESH
CHUNK_HEADS = 4
NT = (((1,), (1,)), ((), ()))
TN = (((0,), (0,)), ((), ()))


def kernel(n, replicas, len_ref, dom_ref, weight_ref, q_hbm, kv_hbm, g_hbm, dq_out, dkv_out,
           q_v, kv_v, g_v, dq_s, dkv_s, counts,
           q_send, q_recv, g_send, g_recv, kv_send, kv_recv, c_send, c_recv,
           dq_send, dq_recv, dkv_send, dkv_recv):
    seq, q_cols = q_v.shape
    span = kv_v.shape[1] // 2
    kv_heads = span // HEAD_SIZE
    group = q_cols // span
    width = min(CHUNK_HEADS, group) * HEAD_SIZE
    chunks = q_cols // width
    per_group = chunks // kv_heads
    inv_root = 1.0 / math.sqrt(HEAD_SIZE)

    me = lax.axis_index("section")
    replica = lax.axis_index("dp")
    half = n // 2
    pair = lax.rem(me + half, n)
    base = lax.div(me, half) * half
    place = me - base
    g_to = base + lax.rem(place + half - 1, half)
    g_from = base + lax.rem(place + 1, half)
    crossed = place == half - 1

    barrier = pltpu.get_barrier_semaphore()
    for other in (pair, g_to, g_from):
        pl.semaphore_signal(barrier, inc=1, device_id={"section": other}, device_id_type=MESH)
    for off in range(1, replicas):
        pl.semaphore_signal(barrier, inc=1, device_id={"dp": lax.rem(replica + off, replicas)},
                            device_id_type=MESH)

    length = len_ref[0]
    domain = dom_ref[0]
    lane = lax.broadcasted_iota(jnp.int32, (8, 128), 1)
    onehot = lane == domain
    counts[0] = jnp.where(onehot, length, 0)

    def cols(c):
        return pl.ds(pl.multiple_of(c * width, width), width)

    def remote(src, dst, send, recv, **to):
        return pltpu.make_async_remote_copy(src_ref=src, dst_ref=dst, send_sem=send, recv_sem=recv,
                                            device_id=to, device_id_type=MESH)

    def q_copy(c):
        return remote(q_hbm.at[0, 0, :, cols(c)], q_v.at[:, cols(c)], q_send.at[c], q_recv.at[c],
                      section=pair)

    def q_local(c):
        return pltpu.make_async_copy(q_hbm.at[0, 0, :, cols(c)], q_v.at[:, cols(c)], q_recv.at[c])

    def g_copy(c):
        return remote(g_hbm.at[0, 0, :, cols(c)], g_v.at[:, cols(c)], g_send.at[c], g_recv.at[c],
                      section=g_to)

    def dq_copy(c):
        return remote(dq_s.at[:, cols(c)], dq_out.at[0, 0, :, cols(c)], dq_send.at[c], dq_recv.at[c],
                      section=pair)

    def dq_local(c):
        return pltpu.make_async_copy(dq_s.at[:, cols(c)], dq_out.at[0, 0, :, cols(c)], dq_send.at[c])

    kv_copy = remote(kv_hbm.at[0, 0], kv_v, kv_send, kv_recv, section=pair)
    kv_local = pltpu.make_async_copy(kv_hbm.at[0, 0], kv_v, kv_recv)
    dkv_copy = remote(dkv_s, dkv_out.at[0, 0], dkv_send, dkv_recv, section=pair)
    dkv_local = pltpu.make_async_copy(dkv_s, dkv_out.at[0, 0], dkv_send)
    count_copies = [
        remote(counts.at[0], counts.at[off], c_send.at[off], c_recv.at[off],
               dp=lax.rem(replica + off, replicas))
        for off in range(1, replicas)
    ]

    @pl.when(crossed)
    def _():
        kv_local.start()
        for c in range(chunks):
            q_local(c).start()

    pl.semaphore_wait(barrier, 3 + replicas - 1)

    @pl.when(jnp.logical_not(crossed))
    def _():
        kv_copy.start()

    for copy in count_copies:
        copy.start()
    for c in range(chunks):
        g_copy(c).start()

        @pl.when(jnp.logical_not(crossed))
        def _():
            q_copy(c).start()

    weight = jnp.float32(0.0)
    for d in range(DOMAINS):
        weight = jnp.where(domain == d, weight_ref[d], weight)
    for copy in count_copies:
        copy.wait()
    total = counts[0, 0:1]
    for off in range(1, replicas):
        total = total + counts[off, 0:1]
    total = total.astype(jnp.float32)
    own = jnp.sum(jnp.where(onehot[0:1], total, 0.0), axis=1, keepdims=True)
    factor = weight * jnp.sum(total, axis=1, keepdims=True) / (DOMAINS * own)

    key_row = lax.broadcasted_iota(jnp.int32, (seq, seq), 0)
    query_col = lax.broadcasted_iota(jnp.int32, (seq, seq), 1)
    allowed = (key_row <= query_col) & (key_row < length)
    live = query_col[0:1] < length

    @pl.when(crossed)
    def _():
        kv_local.wait()

    @pl.when(jnp.logical_not(crossed))
    def _():
        kv_copy.wait_recv()

    def one_group(k, carry):
        at_k = pl.ds(pl.multiple_of(k * HEAD_SIZE, HEAD_SIZE), HEAD_SIZE)
        at_v = pl.ds(pl.multiple_of(span + k * HEAD_SIZE, HEAD_SIZE), HEAD_SIZE)
        key = kv_v[:, at_k]
        value = kv_v[:, at_v]
        d_key = jnp.zeros((seq, HEAD_SIZE), jnp.float32)
        d_value = jnp.zeros((seq, HEAD_SIZE), jnp.float32)
        for sub in range(per_group):
            c = k * per_group + sub
            g_copy(c).wait_recv()

            @pl.when(crossed)
            def _():
                q_local(c).wait()

            @pl.when(jnp.logical_not(crossed))
            def _():
                q_copy(c).wait_recv()

            for h in range(width // HEAD_SIZE):
                at = pl.ds(pl.multiple_of(c * width + h * HEAD_SIZE, HEAD_SIZE), HEAD_SIZE)
                query = q_v[:, at]
                grad = g_v[:, at]
                scores = lax.dot_general(key, query, NT, preferred_element_type=jnp.float32)
                scores = jnp.where(allowed, scores, -1e30)
                peak = jnp.max(scores, axis=0, keepdims=True)
                expo = jnp.exp2((scores - peak) * (inv_root * math.log2(math.e)))
                scale = jnp.where(live, 1.0 / jnp.sum(expo, axis=0, keepdims=True), 0.0)
                prob = expo * scale
                d_prob = lax.dot_general(value, grad, NT, preferred_element_type=jnp.float32)
                row_total = jnp.sum(prob * d_prob, axis=0, keepdims=True)
                d_scores = (prob * (d_prob - row_total) * inv_root).astype(jnp.bfloat16)
                d_value += jnp.dot(prob.astype(jnp.bfloat16), grad, preferred_element_type=jnp.float32)
                d_key += jnp.dot(d_scores, query, preferred_element_type=jnp.float32)
                d_query = lax.dot_general(d_scores, key, TN, preferred_element_type=jnp.float32)
                dq_s[:, at] = (d_query * factor).astype(dq_s.dtype)

            @pl.when(crossed)
            def _():
                dq_copy(c).start()

            @pl.when(jnp.logical_not(crossed))
            def _():
                dq_local(c).start()

        dkv_s[:, at_k] = (d_key * factor).astype(dkv_s.dtype)
        dkv_s[:, at_v] = (d_value * factor).astype(dkv_s.dtype)
        return carry

    lax.fori_loop(0, kv_heads, one_group, 0)

    @pl.when(crossed)
    def _():
        dkv_copy.start()
        for c in range(chunks):
            dq_copy(c).wait()
        dkv_copy.wait()

    @pl.when(jnp.logical_not(crossed))
    def _():
        dkv_local.start()
        kv_copy.wait_send()
        for c in range(chunks):
            q_copy(c).wait_send()
            dq_local(c).wait()
        dkv_local.wait()

    for c in range(chunks):
        g_copy(c).wait_send()


def body(n, replicas, stash_q, stash_kv, upstream, lengths, domains, domain_weight):
    _, _, seq, q_cols = stash_q.shape
    kv_cols = stash_kv.shape[-1]
    group = 2 * q_cols // kv_cols
    chunks = q_cols // (min(CHUNK_HEADS, group) * HEAD_SIZE)
    dma = pltpu.SemaphoreType.DMA
    flops = 5 * 2 * seq * seq * q_cols
    return pl.pallas_call(
        functools.partial(kernel, n, replicas),
        out_shape=(
            jax.ShapeDtypeStruct(stash_q.shape, stash_q.dtype),
            jax.ShapeDtypeStruct(stash_kv.shape, stash_kv.dtype),
        ),
        in_specs=[pl.BlockSpec(memory_space=pltpu.SMEM)] * 3 + [pl.BlockSpec(memory_space=pltpu.HBM)] * 3,
        out_specs=[pl.BlockSpec(memory_space=pl.ANY)] * 2,
        scratch_shapes=[
            pltpu.VMEM((seq, q_cols), jnp.bfloat16),
            pltpu.VMEM((seq, kv_cols), jnp.bfloat16),
            pltpu.VMEM((seq, q_cols), jnp.bfloat16),
            pltpu.VMEM((seq, q_cols), jnp.bfloat16),
            pltpu.VMEM((seq, kv_cols), jnp.bfloat16),
            pltpu.VMEM((replicas, 8, 128), jnp.int32),
            dma((chunks,)), dma((chunks,)), dma((chunks,)), dma((chunks,)),
            dma, dma, dma((replicas,)), dma((replicas,)),
            dma((chunks,)), dma((chunks,)), dma, dma,
        ],
        compiler_params=pltpu.CompilerParams(
            collective_id=0, has_side_effects=True, vmem_limit_bytes=24 * 1024 * 1024
        ),
        cost_estimate=pl.CostEstimate(flops=flops, bytes_accessed=4 * 2 * seq * q_cols, transcendentals=seq * q_cols),
    )(lengths, domains, domain_weight, stash_q, stash_kv, upstream)


def solution(mesh):
    spec = P("section", "dp", None, None)
    return jax.shard_map(
        functools.partial(body, mesh.shape["section"], mesh.shape["dp"]),
        mesh=mesh,
        in_specs=(spec, spec, spec, P("dp"), P("dp"), P()),
        out_specs=(spec, spec),
        check_vma=False,
    )
```

```python
import functools
import math

import jax
import jax.numpy as jnp
from jax import lax
from jax.experimental import pallas as pl
from jax.experimental.pallas import tpu as pltpu
from jax.sharding import PartitionSpec as P

HEAD_SIZE = 128
DOMAINS = 7
MESH = pl.DeviceIdType.MESH
CHUNK_HEADS = 4
NT = (((1,), (1,)), ((), ()))
TN = (((0,), (0,)), ((), ()))


def kernel(n, replicas, len_hbm, dom_hbm, weight_hbm, q_hbm, kv_hbm, g_hbm, dq_out, dkv_out,
           q_v, kv_v, g_v, dq_s, dkv_s, counts, len_ref, dom_ref, weight_ref, scalar_sems,
           q_send, q_recv, g_send, g_recv, kv_send, kv_recv, c_send, c_recv,
           dq_send, dq_recv, dkv_send, dkv_recv):
    seq, q_cols = q_v.shape
    span = kv_v.shape[1] // 2
    kv_heads = span // HEAD_SIZE
    group = q_cols // span
    width = min(CHUNK_HEADS, group) * HEAD_SIZE
    chunks = q_cols // width
    per_group = chunks // kv_heads
    inv_root = 1.0 / math.sqrt(HEAD_SIZE)

    me = lax.axis_index("section")
    replica = lax.axis_index("dp")
    half = n // 2
    pair = lax.rem(me + half, n)
    base = lax.div(me, half) * half
    place = me - base
    g_to = base + lax.rem(place + half - 1, half)
    g_from = base + lax.rem(place + 1, half)
    crossed = place == half - 1

    scalars = [
        pltpu.make_async_copy(src, dst, scalar_sems.at[i])
        for i, (src, dst) in enumerate(
            ((len_hbm, len_ref), (dom_hbm, dom_ref), (weight_hbm, weight_ref)))
    ]
    for copy in scalars:
        copy.start()
    barrier = pltpu.get_barrier_semaphore()
    for other in (pair, g_to, g_from):
        pl.semaphore_signal(barrier, inc=1, device_id={"section": other}, device_id_type=MESH)
    for off in range(1, replicas):
        pl.semaphore_signal(barrier, inc=1, device_id={"dp": lax.rem(replica + off, replicas)},
                            device_id_type=MESH)

    for copy in scalars:
        copy.wait()
    length = len_ref[0]
    domain = dom_ref[0]
    lane = lax.broadcasted_iota(jnp.int32, (8, 128), 1)
    onehot = lane == domain
    counts[0] = jnp.where(onehot, length, 0)

    def cols(c):
        return pl.ds(pl.multiple_of(c * width, width), width)

    def remote(src, dst, send, recv, **to):
        return pltpu.make_async_remote_copy(src_ref=src, dst_ref=dst, send_sem=send, recv_sem=recv,
                                            device_id=to, device_id_type=MESH)

    def q_copy(c):
        return remote(q_hbm.at[0, 0, :, cols(c)], q_v.at[:, cols(c)], q_send.at[c], q_recv.at[c],
                      section=pair)

    def q_local(c):
        return pltpu.make_async_copy(q_hbm.at[0, 0, :, cols(c)], q_v.at[:, cols(c)], q_recv.at[c])

    def g_copy(c):
        return remote(g_hbm.at[0, 0, :, cols(c)], g_v.at[:, cols(c)], g_send.at[c], g_recv.at[c],
                      section=g_to)

    def dq_copy(c):
        return remote(dq_s.at[:, cols(c)], dq_out.at[0, 0, :, cols(c)], dq_send.at[c], dq_recv.at[c],
                      section=pair)

    def dq_local(c):
        return pltpu.make_async_copy(dq_s.at[:, cols(c)], dq_out.at[0, 0, :, cols(c)], dq_send.at[c])

    kv_copy = remote(kv_hbm.at[0, 0], kv_v, kv_send, kv_recv, section=pair)
    kv_local = pltpu.make_async_copy(kv_hbm.at[0, 0], kv_v, kv_recv)
    dkv_copy = remote(dkv_s, dkv_out.at[0, 0], dkv_send, dkv_recv, section=pair)
    dkv_local = pltpu.make_async_copy(dkv_s, dkv_out.at[0, 0], dkv_send)
    count_copies = [
        remote(counts.at[0], counts.at[off], c_send.at[off], c_recv.at[off],
               dp=lax.rem(replica + off, replicas))
        for off in range(1, replicas)
    ]

    @pl.when(crossed)
    def _():
        kv_local.start()
        for c in range(chunks):
            q_local(c).start()

    pl.semaphore_wait(barrier, 3 + replicas - 1)

    @pl.when(jnp.logical_not(crossed))
    def _():
        kv_copy.start()

    for copy in count_copies:
        copy.start()
    for c in range(chunks):
        g_copy(c).start()

        @pl.when(jnp.logical_not(crossed))
        def _():
            q_copy(c).start()

    weight = jnp.float32(0.0)
    for d in range(DOMAINS):
        weight = jnp.where(domain == d, weight_ref[d], weight)
    for copy in count_copies:
        copy.wait()
    total = counts[0, 0:1]
    for off in range(1, replicas):
        total = total + counts[off, 0:1]
    total = total.astype(jnp.float32)
    own = jnp.sum(jnp.where(onehot[0:1], total, 0.0), axis=1, keepdims=True)
    factor = weight * jnp.sum(total, axis=1, keepdims=True) / (DOMAINS * own)

    key_row = lax.broadcasted_iota(jnp.int32, (seq, seq), 0)
    query_col = lax.broadcasted_iota(jnp.int32, (seq, seq), 1)
    allowed = (key_row <= query_col) & (key_row < length)
    live = query_col[0:1] < length

    @pl.when(crossed)
    def _():
        kv_local.wait()

    @pl.when(jnp.logical_not(crossed))
    def _():
        kv_copy.wait_recv()

    def one_group(k, carry):
        at_k = pl.ds(pl.multiple_of(k * HEAD_SIZE, HEAD_SIZE), HEAD_SIZE)
        at_v = pl.ds(pl.multiple_of(span + k * HEAD_SIZE, HEAD_SIZE), HEAD_SIZE)
        key = kv_v[:, at_k]
        value = kv_v[:, at_v]
        d_key = jnp.zeros((seq, HEAD_SIZE), jnp.float32)
        d_value = jnp.zeros((seq, HEAD_SIZE), jnp.float32)
        for sub in range(per_group):
            c = k * per_group + sub
            g_copy(c).wait_recv()

            @pl.when(crossed)
            def _():
                q_local(c).wait()

            @pl.when(jnp.logical_not(crossed))
            def _():
                q_copy(c).wait_recv()

            for h in range(width // HEAD_SIZE):
                at = pl.ds(pl.multiple_of(c * width + h * HEAD_SIZE, HEAD_SIZE), HEAD_SIZE)
                query = q_v[:, at]
                grad = g_v[:, at]
                scores = lax.dot_general(key, query, NT, preferred_element_type=jnp.float32)
                scores = jnp.where(allowed, scores, -1e30)
                peak = jnp.max(scores, axis=0, keepdims=True)
                expo = jnp.exp2((scores - peak) * (inv_root * math.log2(math.e)))
                scale = jnp.where(live, 1.0 / jnp.sum(expo, axis=0, keepdims=True), 0.0)
                prob = expo * scale
                d_prob = lax.dot_general(value, grad, NT, preferred_element_type=jnp.float32)
                row_total = jnp.sum(prob * d_prob, axis=0, keepdims=True)
                d_scores = (prob * (d_prob - row_total) * inv_root).astype(jnp.bfloat16)
                d_value += jnp.dot(prob.astype(jnp.bfloat16), grad, preferred_element_type=jnp.float32)
                d_key += jnp.dot(d_scores, query, preferred_element_type=jnp.float32)
                d_query = lax.dot_general(d_scores, key, TN, preferred_element_type=jnp.float32)
                dq_s[:, at] = (d_query * factor).astype(dq_s.dtype)

            @pl.when(crossed)
            def _():
                dq_copy(c).start()

            @pl.when(jnp.logical_not(crossed))
            def _():
                dq_local(c).start()

        dkv_s[:, at_k] = (d_key * factor).astype(dkv_s.dtype)
        dkv_s[:, at_v] = (d_value * factor).astype(dkv_s.dtype)
        return carry

    lax.fori_loop(0, kv_heads, one_group, 0)

    @pl.when(crossed)
    def _():
        dkv_copy.start()
        for c in range(chunks):
            dq_copy(c).wait()
        dkv_copy.wait()

    @pl.when(jnp.logical_not(crossed))
    def _():
        dkv_local.start()
        kv_copy.wait_send()
        for c in range(chunks):
            q_copy(c).wait_send()
            dq_local(c).wait()
        dkv_local.wait()

    for c in range(chunks):
        g_copy(c).wait_send()


def store(dq_in, dkv_in, dq_out, dkv_out, sems):
    copies = [pltpu.make_async_copy(dq_in, dq_out, sems.at[0]), pltpu.make_async_copy(dkv_in, dkv_out, sems.at[1])]
    for copy in copies:
        copy.start()
    for copy in copies:
        copy.wait()


def body(n, replicas, stash_q, stash_kv, upstream, lengths, domains, domain_weight):
    _, _, seq, q_cols = stash_q.shape
    kv_cols = stash_kv.shape[-1]
    group = 2 * q_cols // kv_cols
    chunks = q_cols // (min(CHUNK_HEADS, group) * HEAD_SIZE)
    dma = pltpu.SemaphoreType.DMA
    flops = 5 * 2 * seq * seq * q_cols
    args = [pltpu.with_memory_space_constraint(x, pltpu.HBM)
            for x in (domain_weight, stash_q, stash_kv, upstream)]
    results = pl.pallas_call(
        functools.partial(kernel, n, replicas),
        out_shape=(
            jax.ShapeDtypeStruct(stash_q.shape, stash_q.dtype),
            jax.ShapeDtypeStruct(stash_kv.shape, stash_kv.dtype),
        ),
        in_specs=[pl.BlockSpec(memory_space=pl.ANY)] * 6,
        out_specs=[pl.BlockSpec(memory_space=pl.ANY)] * 2,
        scratch_shapes=[
            pltpu.VMEM((seq, q_cols), jnp.bfloat16),
            pltpu.VMEM((seq, kv_cols), jnp.bfloat16),
            pltpu.VMEM((seq, q_cols), jnp.bfloat16),
            pltpu.VMEM((seq, q_cols), jnp.bfloat16),
            pltpu.VMEM((seq, kv_cols), jnp.bfloat16),
            pltpu.VMEM((replicas, 8, 128), jnp.int32),
            pltpu.SMEM((1,), jnp.int32), pltpu.SMEM((1,), jnp.int32), pltpu.SMEM(domain_weight.shape, jnp.float32), dma((3,)),
            dma((chunks,)), dma((chunks,)), dma((chunks,)), dma((chunks,)),
            dma, dma, dma((replicas,)), dma((replicas,)),
            dma((chunks,)), dma((chunks,)), dma, dma,
        ],
        compiler_params=pltpu.CompilerParams(
            collective_id=0, has_side_effects=True, vmem_limit_bytes=24 * 1024 * 1024
        ),
        cost_estimate=pl.CostEstimate(flops=flops, bytes_accessed=4 * 2 * seq * q_cols, transcendentals=seq * q_cols),
    )(lengths, domains, *args)
    results = [pltpu.with_memory_space_constraint(r, pltpu.VMEM) for r in results]
    return pl.pallas_call(
        store,
        out_shape=tuple(jax.ShapeDtypeStruct(r.shape, r.dtype) for r in results),
        in_specs=[pl.BlockSpec(memory_space=pl.ANY)] * 2,
        out_specs=[pl.BlockSpec(memory_space=pl.ANY)] * 2,
        scratch_shapes=[dma((2,))],
    )(*results)


def solution(mesh):
    spec = P("section", "dp", None, None)
    return jax.shard_map(
        functools.partial(body, mesh.shape["section"], mesh.shape["dp"]),
        mesh=mesh,
        in_specs=(spec, spec, spec, P("dp"), P("dp"), P()),
        out_specs=(spec, spec),
        check_vma=False,
    )
```

```python
import functools
import math

import jax
import jax.numpy as jnp
from jax import lax
from jax.experimental import pallas as pl
from jax.experimental.pallas import tpu as pltpu
from jax.sharding import PartitionSpec as P

HEAD_SIZE = 128
DOMAINS = 7
MESH = pl.DeviceIdType.MESH
CHUNK_HEADS = 4
PACED_CHUNKS = 2
NT = (((1,), (1,)), ((), ()))
TN = (((0,), (0,)), ((), ()))


def kernel(n, replicas, len_hbm, dom_hbm, weight_hbm, q_hbm, kv_hbm, g_hbm, dq_out, dkv_out,
           q_v, kv_v, g_v, dq_s, dkv_s, counts, len_ref, dom_ref, weight_ref, scalar_sems,
           q_send, q_recv, g_send, g_recv, kv_send, kv_recv, c_send, c_recv,
           dq_send, dq_recv, dkv_send, dkv_recv):
    seq, q_cols = q_v.shape
    span = kv_v.shape[1] // 2
    kv_heads = span // HEAD_SIZE
    group = q_cols // span
    width = min(CHUNK_HEADS, group) * HEAD_SIZE
    chunks = q_cols // width
    per_group = chunks // kv_heads
    inv_root = 1.0 / math.sqrt(HEAD_SIZE)

    me = lax.axis_index("section")
    replica = lax.axis_index("dp")
    half = n // 2
    pair = lax.rem(me + half, n)
    base = lax.div(me, half) * half
    place = me - base
    g_to = base + lax.rem(place + half - 1, half)
    g_from = base + lax.rem(place + 1, half)
    crossed = place == half - 1
    paced = (lax.rem(place, 2) == 1) & jnp.logical_not(crossed)
    free = (lax.rem(place, 2) == 0) & jnp.logical_not(crossed)

    barrier = pltpu.get_barrier_semaphore()
    for other in (pair, g_to, g_from):
        pl.semaphore_signal(barrier, inc=1, device_id={"section": other}, device_id_type=MESH)
    for off in range(1, replicas):
        pl.semaphore_signal(barrier, inc=1, device_id={"dp": lax.rem(replica + off, replicas)},
                            device_id_type=MESH)

    def cols(c):
        return pl.ds(pl.multiple_of(c * width, width), width)

    def remote(src, dst, send, recv, **to):
        return pltpu.make_async_remote_copy(src_ref=src, dst_ref=dst, send_sem=send, recv_sem=recv,
                                            device_id=to, device_id_type=MESH)

    def q_copy(c):
        return remote(q_hbm.at[0, 0, :, cols(c)], q_v.at[:, cols(c)], q_send.at[c], q_recv.at[c],
                      section=pair)

    def q_local(c):
        return pltpu.make_async_copy(q_hbm.at[0, 0, :, cols(c)], q_v.at[:, cols(c)], q_recv.at[c])

    def g_copy(c):
        return remote(g_hbm.at[0, 0, :, cols(c)], g_v.at[:, cols(c)], g_send.at[c], g_recv.at[c],
                      section=g_to)

    def dq_copy(c):
        return remote(dq_s.at[:, cols(c)], dq_out.at[0, 0, :, cols(c)], dq_send.at[c], dq_recv.at[c],
                      section=pair)

    def dq_local(c):
        return pltpu.make_async_copy(dq_s.at[:, cols(c)], dq_out.at[0, 0, :, cols(c)], dq_send.at[c])

    kv_copy = remote(kv_hbm.at[0, 0], kv_v, kv_send, kv_recv, section=pair)
    kv_local = pltpu.make_async_copy(kv_hbm.at[0, 0], kv_v, kv_recv)
    dkv_copy = remote(dkv_s, dkv_out.at[0, 0], dkv_send, dkv_recv, section=pair)
    dkv_local = pltpu.make_async_copy(dkv_s, dkv_out.at[0, 0], dkv_send)
    count_copies = [
        remote(counts.at[0], counts.at[off], c_send.at[off], c_recv.at[off],
               dp=lax.rem(replica + off, replicas))
        for off in range(1, replicas)
    ]

    scalars = [
        pltpu.make_async_copy(src, dst, scalar_sems.at[i])
        for i, (src, dst) in enumerate(
            ((len_hbm, len_ref), (dom_hbm, dom_ref), (weight_hbm, weight_ref)))
    ]
    for copy in scalars:
        copy.start()

    pl.semaphore_wait(barrier, 3 + replicas - 1)

    @pl.when(crossed)
    def _():
        kv_local.start()
        for c in range(chunks):
            q_local(c).start()

    @pl.when(jnp.logical_not(crossed))
    def _():
        kv_copy.start()

    for c in range(chunks):
        g_copy(c).start()

        @pl.when(free | (paced & (c < 1)))
        def _():
            q_copy(c).start()

    for copy in scalars:
        copy.wait()
    length = len_ref[0]
    domain = dom_ref[0]
    lane = lax.broadcasted_iota(jnp.int32, (8, 128), 1)
    onehot = lane == domain
    counts[0] = jnp.where(onehot, length, 0)

    for copy in count_copies:
        copy.start()

    weight = jnp.float32(0.0)
    for d in range(DOMAINS):
        weight = jnp.where(domain == d, weight_ref[d], weight)
    for copy in count_copies:
        copy.wait()
    total = counts[0, 0:1]
    for off in range(1, replicas):
        total = total + counts[off, 0:1]
    total = total.astype(jnp.float32)
    own = jnp.sum(jnp.where(onehot[0:1], total, 0.0), axis=1, keepdims=True)
    factor = weight * jnp.sum(total, axis=1, keepdims=True) / (DOMAINS * own)

    key_row = lax.broadcasted_iota(jnp.int32, (seq, seq), 0)
    query_col = lax.broadcasted_iota(jnp.int32, (seq, seq), 1)
    allowed = (key_row <= query_col) & (key_row < length)
    live = query_col[0:1] < length

    @pl.when(crossed)
    def _():
        kv_local.wait()

    @pl.when(jnp.logical_not(crossed))
    def _():
        kv_copy.wait_recv()

    def one_group(k, carry):
        at_k = pl.ds(pl.multiple_of(k * HEAD_SIZE, HEAD_SIZE), HEAD_SIZE)
        at_v = pl.ds(pl.multiple_of(span + k * HEAD_SIZE, HEAD_SIZE), HEAD_SIZE)
        key = kv_v[:, at_k]
        value = kv_v[:, at_v]
        d_key = jnp.zeros((seq, HEAD_SIZE), jnp.float32)
        d_value = jnp.zeros((seq, HEAD_SIZE), jnp.float32)
        for sub in range(per_group):
            c = k * per_group + sub
            g_copy(c).wait_recv()

            @pl.when(crossed)
            def _():
                q_local(c).wait()

            @pl.when(jnp.logical_not(crossed))
            def _():
                q_copy(c).wait_recv()
                q_copy(c).wait_send()

            @pl.when(paced & (c < PACED_CHUNKS - 1))
            def _():
                q_copy(c + 1).start()

            @pl.when(paced & (c == PACED_CHUNKS - 1))
            def _():
                for later in range(PACED_CHUNKS, chunks):
                    q_copy(later).start()

            for h in range(width // HEAD_SIZE):
                at = pl.ds(pl.multiple_of(c * width + h * HEAD_SIZE, HEAD_SIZE), HEAD_SIZE)
                query = q_v[:, at]
                grad = g_v[:, at]
                scores = lax.dot_general(key, query, NT, preferred_element_type=jnp.float32)
                scores = jnp.where(allowed, scores, -1e30)
                peak = jnp.max(scores, axis=0, keepdims=True)
                expo = jnp.exp2((scores - peak) * (inv_root * math.log2(math.e)))
                scale = jnp.where(live, 1.0 / jnp.sum(expo, axis=0, keepdims=True), 0.0)
                prob = expo * scale
                d_prob = lax.dot_general(value, grad, NT, preferred_element_type=jnp.float32)
                row_total = jnp.sum(prob * d_prob, axis=0, keepdims=True)
                d_scores = (prob * (d_prob - row_total) * inv_root).astype(jnp.bfloat16)
                d_value += jnp.dot(prob.astype(jnp.bfloat16), grad, preferred_element_type=jnp.float32)
                d_key += jnp.dot(d_scores, query, preferred_element_type=jnp.float32)
                d_query = lax.dot_general(d_scores, key, TN, preferred_element_type=jnp.float32)
                dq_s[:, at] = (d_query * factor).astype(dq_s.dtype)

            @pl.when(crossed)
            def _():
                dq_copy(c).start()

            @pl.when(jnp.logical_not(crossed))
            def _():
                dq_local(c).start()

        dkv_s[:, at_k] = (d_key * factor).astype(dkv_s.dtype)
        dkv_s[:, at_v] = (d_value * factor).astype(dkv_s.dtype)
        return carry

    lax.fori_loop(0, kv_heads, one_group, 0)

    @pl.when(crossed)
    def _():
        dkv_copy.start()
        for c in range(chunks):
            dq_copy(c).wait()
        dkv_copy.wait()

    @pl.when(jnp.logical_not(crossed))
    def _():
        dkv_local.start()
        kv_copy.wait_send()
        for c in range(chunks):
            dq_local(c).wait()
        dkv_local.wait()

    for c in range(chunks):
        g_copy(c).wait_send()


def store(dq_in, dkv_in, dq_out, dkv_out, sems):
    copies = [pltpu.make_async_copy(dq_in, dq_out, sems.at[0]), pltpu.make_async_copy(dkv_in, dkv_out, sems.at[1])]
    for copy in copies:
        copy.start()
    for copy in copies:
        copy.wait()


def body(n, replicas, stash_q, stash_kv, upstream, lengths, domains, domain_weight):
    _, _, seq, q_cols = stash_q.shape
    kv_cols = stash_kv.shape[-1]
    group = 2 * q_cols // kv_cols
    chunks = q_cols // (min(CHUNK_HEADS, group) * HEAD_SIZE)
    dma = pltpu.SemaphoreType.DMA
    flops = 5 * 2 * seq * seq * q_cols
    args = [pltpu.with_memory_space_constraint(x, pltpu.HBM)
            for x in (domain_weight, stash_q, stash_kv, upstream)]
    results = pl.pallas_call(
        functools.partial(kernel, n, replicas),
        out_shape=(
            jax.ShapeDtypeStruct(stash_q.shape, stash_q.dtype),
            jax.ShapeDtypeStruct(stash_kv.shape, stash_kv.dtype),
        ),
        in_specs=[pl.BlockSpec(memory_space=pl.ANY)] * 6,
        out_specs=[pl.BlockSpec(memory_space=pl.ANY)] * 2,
        scratch_shapes=[
            pltpu.VMEM((seq, q_cols), jnp.bfloat16),
            pltpu.VMEM((seq, kv_cols), jnp.bfloat16),
            pltpu.VMEM((seq, q_cols), jnp.bfloat16),
            pltpu.VMEM((seq, q_cols), jnp.bfloat16),
            pltpu.VMEM((seq, kv_cols), jnp.bfloat16),
            pltpu.VMEM((replicas, 8, 128), jnp.int32),
            pltpu.SMEM((1,), jnp.int32), pltpu.SMEM((1,), jnp.int32), pltpu.SMEM(domain_weight.shape, jnp.float32), dma((3,)),
            dma((chunks,)), dma((chunks,)), dma((chunks,)), dma((chunks,)),
            dma, dma, dma((replicas,)), dma((replicas,)),
            dma((chunks,)), dma((chunks,)), dma, dma,
        ],
        compiler_params=pltpu.CompilerParams(
            collective_id=0, has_side_effects=True, vmem_limit_bytes=24 * 1024 * 1024
        ),
        cost_estimate=pl.CostEstimate(flops=flops, bytes_accessed=4 * 2 * seq * q_cols, transcendentals=seq * q_cols),
    )(lengths, domains, *args)
    results = [pltpu.with_memory_space_constraint(r, pltpu.VMEM) for r in results]
    return pl.pallas_call(
        store,
        out_shape=tuple(jax.ShapeDtypeStruct(r.shape, r.dtype) for r in results),
        in_specs=[pl.BlockSpec(memory_space=pl.ANY)] * 2,
        out_specs=[pl.BlockSpec(memory_space=pl.ANY)] * 2,
        scratch_shapes=[dma((2,))],
    )(*results)


def solution(mesh):
    spec = P("section", "dp", None, None)
    return jax.shard_map(
        functools.partial(body, mesh.shape["section"], mesh.shape["dp"]),
        mesh=mesh,
        in_specs=(spec, spec, spec, P("dp"), P("dp"), P()),
        out_specs=(spec, spec),
        check_vma=False,
    )
```
